512 devices in a mesh: chan: 16 (over x, y_hi, core), tm: 32 (over z, y_lo).
Axes of the slice: x: 4, y: 8 (y_hi: 2, y_lo: 4; y = y_hi * 4 + y_lo), z: 8, core: 2. Of those that a mesh axis runs over, the one named last changes fastest.
Arguments:
- traces: bfloat16 [16, 128, 128, 512], P('chan', 'tm'), may hold values from -6 to 6
- pair_listed: int32 [16, 8], P('chan'), may hold values from 0 to 1, as said below
- owner_slot: int32 [16, 8], P('chan'), may hold values from 0 to 31, as said below
- window_count: int32 [16, 8, 32], P('chan'), may hold values from 1 to 4, as said below
Outputs:
- stacks: float32 [16, 32, 128, 128], P('chan', 'tm')
The draws below stay inside these ranges and needn't reach their ends.
Inputs may be any that keep to these rules, and one draw needn't show every extreme that they name: `pair_listed`: every distance is listed for block 0. `owner_slot`: distinct within each block's row. `window_count`: the windows entering are the first ones of the group; 4 is reached in every draw.
All inputs are finite; a program needn't handle non-finite values.
Results may differ from the reference program's by a relative error of at most 0.015.
Values may be sent and summed in bfloat16 or wider, within the bound.
No kernel may reach another device: no remote copies, remote signals or barrier semaphores. Data moves between devices by JAX's collectives and lax.ppermute only.
A program may use at most 64 MiB of HBM per device.

```python
import math
import jax
import jax.numpy as jnp
from jax import lax

CHANNELS = 128
SAMPLES = 512
BAND = 64
SMOOTH = 16
OFFSETS = 128
LAGS = 128
WINDOWS = 4
BLOCKS = 16
GROUPS = 32
SPAN = 8
PADDED = 256


def draw_pair_listed(key, part):
    rolls = jax.random.randint(key, (BLOCKS, SPAN), 0, 4)
    block_index = jnp.arange(BLOCKS, dtype=jnp.int32)[:, None]
    listed = (rolls > 0) | (block_index == 0)
    return listed.astype(jnp.int32)


def draw_owner_slot(key, part):
    scores = jax.random.randint(key, (BLOCKS, GROUPS), 0, 1 << 20) * GROUPS
    scores = scores + jnp.arange(GROUPS, dtype=jnp.int32)[None, :]
    ordering = jnp.argsort(scores, axis=1)
    return ordering[:, :SPAN].astype(jnp.int32)


def draw_window_count(key, part):
    counts = jax.random.randint(key, (BLOCKS, SPAN, GROUPS), 1, WINDOWS + 1)
    return counts.at[0, 0, 0].set(WINDOWS).astype(jnp.int32)


def steps_of(own_key, shape, cuts, least, top_value):
    level, own = 1.0, jax.random.fold_in(own_key, 6)
    for dim, shards_of in cuts:
        draws = jnp.exp(jax.random.uniform(jax.random.fold_in(own, dim), (shards_of,), jnp.float32, least / len(cuts), top_value / len(cuts)))
        level = level * jnp.repeat(draws, shape[dim] // shards_of).reshape([-1 if axis == dim else 1 for axis in range(len(shape))])
    return level


def gaussian(own_key, extent, width, bound, split=(), held_as=jnp.bfloat16):
    factor_of = steps_of(own_key, extent, split, -0.22, 0.18) if split else 1.0
    result = jax.random.normal(own_key, extent, jnp.float32) * width * factor_of
    return jnp.minimum(jnp.maximum(result, -bound), bound).astype(held_as)


def setup_inputs(seed: int = 0) -> dict:
    key_of = jax.random.split(jax.random.key(seed), 5)
    traces = gaussian(key_of[0], (BLOCKS, GROUPS * WINDOWS, CHANNELS, SAMPLES), 1.0, 6.0, ((0, 16), (1, 32)))
    pair_listed = draw_pair_listed(jax.random.fold_in(key_of[4], 71), 0)
    owner_slot = draw_owner_slot(jax.random.fold_in(key_of[4], 71), 0)
    window_count = draw_window_count(jax.random.fold_in(key_of[4], 71), 0)
    return dict(traces=traces, pair_listed=pair_listed, owner_slot=owner_slot, window_count=window_count)


WATER = 0.1
PRECISE = lax.Precision.HIGHEST

def angles(left_index, right_index, period):
    product = left_index[:, None] * right_index[None, :] % period
    return 2.0 * math.pi / period * product.astype(jnp.float32)

def smooth_matrix():
    source = jnp.arange(BAND, dtype=jnp.int32)[:, None]
    target = jnp.arange(BAND, dtype=jnp.int32)[None, :]
    start = jnp.clip(target - SMOOTH // 2, 0, BAND - SMOOTH)
    inside = (source >= start) & (source < start + SMOOTH)
    return inside.astype(jnp.float32) / SMOOTH

def whiten_block(block_traces):
    values = block_traces.astype(jnp.float32)
    spectrum = jnp.fft.rfft(values, axis=-1)[..., 1:BAND + 1]
    real_part = jnp.real(spectrum).astype(jnp.float32)
    imag_part = jnp.imag(spectrum).astype(jnp.float32)
    amplitude = jnp.sqrt(real_part * real_part + imag_part * imag_part)
    flat_rows = amplitude.reshape(-1, BAND)
    local_mean = jnp.dot(flat_rows, smooth_matrix(), precision=PRECISE)
    water_level = local_mean + WATER * lax.optimization_barrier(jnp.mean(flat_rows, axis=1, keepdims=True)) + 1e-06
    water_level = water_level.reshape(amplitude.shape)
    return jnp.concatenate([real_part / water_level, imag_part / water_level], axis=-1).astype(jnp.bfloat16)

def channel_fft(block_data):
    complex_values = block_data[..., :BAND].astype(jnp.float32) + 1j * block_data[..., BAND:].astype(jnp.float32)
    return jnp.fft.fft(complex_values, n=PADDED, axis=1)

def reference(traces, pair_listed, owner_slot, window_count):
    whitened = lax.map(whiten_block, traces)
    band_bins = jnp.arange(BAND, dtype=jnp.int32) + 1
    lag_steps = jnp.arange(LAGS, dtype=jnp.int32) - LAGS // 2
    lag_angle = angles(band_bins, lag_steps, SAMPLES)
    lag_cos = jnp.cos(lag_angle)
    lag_sin = jnp.sin(lag_angle)
    offset_rows = (jnp.arange(OFFSETS, dtype=jnp.int32) - OFFSETS // 2) % PADDED
    window_index = jnp.arange(GROUPS * WINDOWS, dtype=jnp.int32)

    def block_stack(block_index):
        own_spectrum = channel_fft(whitened[block_index])
        lagged_all = []
        for distance in range(1, SPAN + 1):
            source = whitened[(block_index - distance) % BLOCKS]
            source_spectrum = channel_fft(source)
            counts = window_count[block_index, distance - 1]
            window_keep = (window_index % WINDOWS < counts[window_index // WINDOWS]).astype(jnp.float32)
            summed = lax.optimization_barrier(jnp.sum(window_keep[:, None, None] * jnp.conj(source_spectrum) * own_spectrum, axis=0))
            correlation = jnp.fft.ifft(summed, axis=0)[offset_rows]
            corr_real = jnp.real(correlation).astype(jnp.float32)
            corr_imag = jnp.imag(correlation).astype(jnp.float32)
            weight = pair_listed[block_index, distance - 1].astype(jnp.float32) / jnp.sum(counts).astype(jnp.float32)
            lagged = jnp.dot(corr_real, lag_cos, precision=PRECISE) - jnp.dot(corr_imag, lag_sin, precision=PRECISE)
            lagged_all.append(lagged * (weight / math.sqrt(BAND)))
        lagged_stack = jnp.stack(lagged_all).reshape(SPAN, -1)
        owner_mask = (owner_slot[block_index][None, :] == jnp.arange(GROUPS, dtype=jnp.int32)[:, None]).astype(jnp.float32)
        placed = jnp.dot(owner_mask, lagged_stack, precision=PRECISE)
        return placed.reshape(GROUPS, OFFSETS, LAGS)
    return lax.map(block_stack, jnp.arange(BLOCKS, dtype=jnp.int32))
```

```python
import math

import jax
import jax.numpy as jnp
import ml_dtypes
import numpy as np
from jax import lax
from jax.experimental import pallas as pl
from jax.experimental.pallas import tpu as pltpu
from jax.sharding import Mesh
from jax.sharding import PartitionSpec as P

BAND = 64
SMOOTH = 16
OFFSETS = 128
LAGS = 128
WATER = 0.1
CHANNELS = 128
SAMPLES = 512
PADDED = 256
WINDOWS = 4
BLOCKS = 16
GROUPS = 32
SPAN = 8
PLANE_GROUPS = 4
CHUNK = 10
EXTENDED = BLOCKS + SPAN

CHAN = ("x", "yh", "core")
TM = ("z", "yl")
PLANE = ("yl",) + CHAN
WHOLE = TM + CHAN
F32 = jnp.float32
BF16 = jnp.bfloat16


def angles(left, right, period):
    return 2.0 * np.pi / period * ((left[:, None] * right[None, :]) % period)


def split_table(table):
    table = table.astype(np.float32)
    high = table.astype(ml_dtypes.bfloat16)
    low = (table - high.astype(np.float32)).astype(ml_dtypes.bfloat16)
    return high, low


def band_table():
    turn = angles(np.arange(BAND) + 1, np.arange(SAMPLES), SAMPLES)
    high, low = split_table(np.concatenate([np.cos(turn), -np.sin(turn)], axis=0))
    return np.concatenate([high, low], axis=0)


def smooth_table():
    source = np.arange(BAND)[None, :]
    start = np.clip(np.arange(BAND)[:, None] - SMOOTH // 2, 0, BAND - SMOOTH)
    inside = (source >= start) & (source < start + SMOOTH)
    return np.concatenate([inside, np.ones_like(inside)], axis=0).astype(ml_dtypes.bfloat16)


def channel_table():
    turn = angles(np.arange(CHANNELS), np.arange(PADDED), PADDED)
    top = np.concatenate([np.cos(turn), -np.sin(turn)], axis=1)
    bottom = np.concatenate([np.sin(turn), np.cos(turn)], axis=1)
    return split_table(np.concatenate([top, bottom], axis=0))


def offset_table():
    turn = angles(np.arange(PADDED), np.arange(OFFSETS) - OFFSETS // 2, PADDED)
    top = np.concatenate([np.cos(turn), np.sin(turn)], axis=1)
    bottom = np.concatenate([-np.sin(turn), np.cos(turn)], axis=1)
    return split_table(np.concatenate([top, bottom], axis=0) / PADDED)


def lag_table():
    turn = angles(np.arange(BAND) + 1, np.arange(LAGS) - LAGS // 2, SAMPLES)
    pair = np.stack([np.cos(turn), -np.sin(turn)], axis=1).reshape(2 * BAND, LAGS)
    return split_table(pair / math.sqrt(BAND))


def dot(left, right):
    return jnp.dot(left, right, preferred_element_type=F32)


def split(value):
    high = value.astype(BF16)
    return high, (value - high.astype(F32)).astype(BF16)


def dot_split(value, table_high, table_low):
    high, low = split(value)
    return dot(high, table_high) + (dot(low, table_high) + dot(high, table_low))


def whiten_kernel(place, owners, counts, traces, table, smooth, out, rows):
    flat = traces[...].reshape(WINDOWS * CHANNELS, SAMPLES)
    both = lax.dot_general(
        table[...], flat, (((1,), (1,)), ((), ())), preferred_element_type=F32
    )
    spectrum = both[: 2 * BAND] + both[2 * BAND :]
    real_part = spectrum[:BAND]
    imag_part = spectrum[BAND:]
    amplitude = jnp.sqrt(real_part * real_part + imag_part * imag_part)
    high, low = split(amplitude)
    sums = dot(smooth[...], high) + dot(smooth[...], low)
    water_level = sums[:BAND] / SMOOTH + WATER * (sums[BAND:] / BAND) + 1e-6
    real_part = real_part / water_level
    imag_part = imag_part / water_level
    for window in range(WINDOWS):
        here = slice(window * CHANNELS, (window + 1) * CHANNELS)
        rows[pl.ds(window, BAND, stride=CHUNK), :] = real_part[:, here]
        rows[pl.ds(WINDOWS + window, BAND, stride=CHUNK), :] = imag_part[:, here]
    lane = lax.broadcasted_iota(jnp.int32, (8, CHANNELS), 1)
    count_row = jnp.zeros((8, CHANNELS), jnp.int32)
    owner_row = jnp.zeros((8, CHANNELS), jnp.int32)
    for step in range(SPAN):
        count_row = jnp.where(lane == step, counts[step, place[0]], count_row)
        owner_row = jnp.where(lane == step, owners[0, step], owner_row)
    count_row = count_row.astype(F32)
    owner_row = owner_row.astype(F32)
    for part in range(BAND // 8):
        rows[pl.ds(part * 8 * CHUNK + 8, 8, stride=CHUNK), :] = count_row
        rows[pl.ds(part * 8 * CHUNK + 9, 8, stride=CHUNK), :] = owner_row
    out[...] = rows[...].astype(BF16)


def cross_kernel(
    chunks, to_high, to_low, back_high, back_low, out, rows, stacked, spectra, cross, slots
):
    rows[...] = chunks[...].astype(F32)
    block_rows = BLOCKS * CHUNK
    for group in range(PLANE_GROUPS):
        for window in range(WINDOWS):
            base = (group * WINDOWS + window) * EXTENDED
            for part in range(2):
                start = group * block_rows + part * WINDOWS + window
                lanes = slice(part * CHANNELS, (part + 1) * CHANNELS)
                stacked[base : base + 8, lanes] = rows[
                    pl.ds(start + 8 * CHUNK, 8, stride=CHUNK), :
                ]
                stacked[base + 8 : base + 24, lanes] = rows[pl.ds(start, 16, stride=CHUNK), :]
    block_data = stacked[...].astype(BF16)
    both = dot(block_data, to_high[...]) + dot(block_data, to_low[...])
    for tile in range(4):
        spectra[tile] = both[:, tile * 128 : (tile + 1) * 128]
    counts = [
        rows[pl.ds(group * block_rows + 8, 16, stride=CHUNK), :] for group in range(PLANE_GROUPS)
    ]
    owners = rows[pl.ds(9, 16, stride=CHUNK), :]
    for step in range(SPAN):
        distance = step + 1
        limits = [
            jnp.broadcast_to(counts[group][:, step : step + 1], (BLOCKS, 128))
            for group in range(PLANE_GROUPS)
        ]
        for half in range(2):
            total_real = jnp.zeros((BLOCKS, 128), F32)
            total_imag = jnp.zeros((BLOCKS, 128), F32)
            for group in range(PLANE_GROUPS):
                for window in range(WINDOWS):
                    base = (group * WINDOWS + window) * EXTENDED + SPAN
                    own = slice(base, base + BLOCKS)
                    before = slice(base - distance, base - distance + BLOCKS)
                    own_real = spectra[half, own, :]
                    own_imag = spectra[2 + half, own, :]
                    src_real = spectra[half, before, :]
                    src_imag = spectra[2 + half, before, :]
                    term_real = src_real * own_real + src_imag * own_imag
                    term_imag = src_real * own_imag - src_imag * own_real
                    keep = limits[group] > float(window)
                    total_real = total_real + jnp.where(keep, term_real, 0.0)
                    total_imag = total_imag + jnp.where(keep, term_imag, 0.0)
            here = slice(step * BLOCKS, (step + 1) * BLOCKS)
            cross[here, half * 128 : (half + 1) * 128] = total_real
            cross[here, PADDED + half * 128 : PADDED + (half + 1) * 128] = total_imag
    partial = dot_split(cross[...], back_high[...], back_low[...])
    owner_of = [
        jnp.broadcast_to(owners[:, step : step + 1], (BLOCKS, 128)) for step in range(SPAN)
    ]
    for owner in range(GROUPS):
        halves = [jnp.zeros((BLOCKS, 128), F32), jnp.zeros((BLOCKS, 128), F32)]
        for step in range(SPAN):
            chosen = owner_of[step] == float(owner)
            for half in range(2):
                piece = partial[
                    step * BLOCKS : (step + 1) * BLOCKS, half * 128 : (half + 1) * 128
                ]
                halves[half] = jnp.where(chosen, piece, halves[half])
        for half in range(2):
            slots[pl.ds(owner * 2 * BLOCKS + half, BLOCKS, stride=2), :] = halves[half]
    out[...] = slots[...].astype(BF16)


def lag_kernel(place, listed, owners, counts, arrived, table_high, table_low, out):
    mine = jnp.int32(0)
    found = jnp.int32(0)
    for step in range(SPAN):
        here = owners[0, step] == place[0]
        mine = jnp.where(here, step, mine)
        found = jnp.where(here, listed[0, step], found)
    total = jnp.int32(0)
    for group in range(GROUPS):
        total = total + counts[mine, group]
    weight = jnp.full((8, LAGS), found, jnp.int32).astype(F32) / jnp.full(
        (8, LAGS), total, jnp.int32
    ).astype(F32)
    summed = arrived[: 2 * BAND].astype(F32)
    for layer in range(1, 8):
        summed = summed + arrived[layer * 2 * BAND : (layer + 1) * 2 * BAND].astype(F32)
    lagged = dot_split(summed.T, table_high[...], table_low[...])
    out[...] = lagged * weight[:1]


def shards(traces, pair_listed, owner_slot, window_count):
    vmem = pl.BlockSpec(memory_space=pltpu.VMEM)
    smem = pl.BlockSpec(memory_space=pltpu.SMEM)
    place = lax.axis_index(TM).astype(jnp.int32).reshape(1)
    counts = window_count[0]
    chunks = pl.pallas_call(
        whiten_kernel,
        out_shape=jax.ShapeDtypeStruct((BAND * CHUNK, CHANNELS), BF16),
        in_specs=[smem, smem, smem, vmem, vmem, vmem],
        out_specs=vmem,
        scratch_shapes=[pltpu.VMEM((BAND * CHUNK, CHANNELS), F32)],
        compiler_params=pltpu.CompilerParams(vmem_limit_bytes=32 << 20),
        name="whiten",
    )(place, owner_slot, counts, traces[0], band_table(), smooth_table())
    chunks = chunks.reshape(BAND, CHUNK // 2, 2, CHANNELS)
    chunks = lax.all_to_all(chunks, PLANE, 0, 0, tiled=True)
    chunks = chunks.reshape(BAND * CHUNK, CHANNELS)
    slots = pl.pallas_call(
        cross_kernel,
        out_shape=jax.ShapeDtypeStruct((GROUPS * BLOCKS * 2, OFFSETS), BF16),
        in_specs=[vmem] * 5,
        out_specs=vmem,
        scratch_shapes=[
            pltpu.VMEM((BAND * CHUNK, CHANNELS), F32),
            pltpu.VMEM((PLANE_GROUPS * WINDOWS * EXTENDED, 2 * CHANNELS), F32),
            pltpu.VMEM((4, PLANE_GROUPS * WINDOWS * EXTENDED, 128), F32),
            pltpu.VMEM((SPAN * BLOCKS, 2 * PADDED), F32),
            pltpu.VMEM((GROUPS * BLOCKS * 2, OFFSETS), F32),
        ],
        compiler_params=pltpu.CompilerParams(vmem_limit_bytes=32 << 20),
        name="cross",
    )(chunks, *channel_table(), *offset_table())
    slots = slots.reshape(GROUPS * BLOCKS, 2, OFFSETS)
    slots = lax.all_to_all(slots, WHOLE, 0, 0, tiled=True)
    slots = slots.reshape(GROUPS * BLOCKS * 2, OFFSETS)
    stacked = pl.pallas_call(
        lag_kernel,
        out_shape=jax.ShapeDtypeStruct((OFFSETS, LAGS), F32),
        in_specs=[smem, smem, smem, smem, vmem, vmem, vmem],
        out_specs=vmem,
        compiler_params=pltpu.CompilerParams(vmem_limit_bytes=32 << 20),
        name="lag",
    )(place, pair_listed, owner_slot, counts, slots, *lag_table())
    return stacked[None, None]


def solution(mesh):
    fine = Mesh(mesh.devices.reshape(4, 2, 2, 8, 4), CHAN + TM)
    placed = (
        P(CHAN, TM, None, None),
        P(CHAN, None),
        P(CHAN, None),
        P(CHAN, None, None),
    )
    return jax.shard_map(
        shards, mesh=fine, in_specs=placed, out_specs=P(CHAN, TM, None, None), check_vma=False
    )
```

```python
import math

import jax
import jax.numpy as jnp
import ml_dtypes
import numpy as np
from jax import lax
from jax.experimental import pallas as pl
from jax.experimental.pallas import tpu as pltpu
from jax.sharding import Mesh
from jax.sharding import PartitionSpec as P

BAND = 64
SMOOTH = 16
OFFSETS = 128
LAGS = 128
WATER = 0.1
CHANNELS = 128
SAMPLES = 512
PADDED = 256
WINDOWS = 4
BLOCKS = 16
GROUPS = 32
SPAN = 8
PLANE_GROUPS = 4
CHUNK = 10
EXTENDED = BLOCKS + SPAN

CHAN = ("x", "yh", "core")
TM = ("z", "yl")
PLANE = ("yl",) + CHAN
WHOLE = TM + CHAN
F32 = jnp.float32
BF16 = jnp.bfloat16


def angles(left, right, period):
    return 2.0 * np.pi / period * ((left[:, None] * right[None, :]) % period)


def split_table(table):
    table = table.astype(np.float32)
    high = table.astype(ml_dtypes.bfloat16)
    low = (table - high.astype(np.float32)).astype(ml_dtypes.bfloat16)
    return high, low


def band_table():
    turn = angles(np.arange(BAND) + 1, np.arange(SAMPLES), SAMPLES)
    high, low = split_table(np.concatenate([np.cos(turn), -np.sin(turn)], axis=0))
    return np.concatenate([high, low], axis=0)


def channel_table():
    turn = angles(np.arange(CHANNELS), np.arange(PADDED), PADDED)
    top = np.concatenate([np.cos(turn), -np.sin(turn)], axis=1)
    bottom = np.concatenate([np.sin(turn), np.cos(turn)], axis=1)
    return split_table(np.concatenate([top, bottom], axis=0))


def offset_table():
    turn = angles(np.arange(PADDED), np.arange(OFFSETS) - OFFSETS // 2, PADDED)
    top = np.concatenate([np.cos(turn), np.sin(turn)], axis=1)
    bottom = np.concatenate([-np.sin(turn), np.cos(turn)], axis=1)
    return split_table(np.concatenate([top, bottom], axis=0) / PADDED)


def lag_table():
    turn = angles(np.arange(BAND) + 1, np.arange(LAGS) - LAGS // 2, SAMPLES)
    pair = np.stack([np.cos(turn), -np.sin(turn)], axis=1).reshape(2 * BAND, LAGS)
    return split_table(pair / math.sqrt(BAND))


def dot(left, right):
    return jnp.dot(left, right, preferred_element_type=F32)


def split(value):
    high = value.astype(BF16)
    return high, (value - high.astype(F32)).astype(BF16)


def dot_split(value, table_high, table_low):
    high, low = split(value)
    return dot(high, table_high) + (dot(low, table_high) + dot(high, table_low))


def smooth_sums(amplitude):
    target = lax.broadcasted_iota(jnp.int32, (2 * BAND, BAND), 0)
    source = lax.broadcasted_iota(jnp.int32, (2 * BAND, BAND), 1)
    start = jnp.clip(target - SMOOTH // 2, 0, BAND - SMOOTH)
    inside = (target >= BAND) | ((source >= start) & (source < start + SMOOTH))
    smooth = inside.astype(F32).astype(BF16)
    high, low = split(amplitude)
    sums = dot(smooth, high) + dot(smooth, low)
    return sums[:BAND], sums[BAND:]


def whiten_kernel(
    place,
    listed_hbm,
    owners_hbm,
    counts_hbm,
    traces_hbm,
    table_hbm,
    out,
    weight,
    listed,
    owners,
    counts,
    traces,
    table,
    rows,
    small_sems,
    table_sem,
    trace_sems,
):
    small = [
        pltpu.make_async_copy(source, target, small_sems.at[k])
        for k, (source, target) in enumerate(
            ((listed_hbm, listed), (owners_hbm, owners), (counts_hbm, counts))
        )
    ]
    whole_table = pltpu.make_async_copy(table_hbm, table, table_sem)
    parts = [
        pltpu.make_async_copy(traces_hbm.at[window], traces.at[window], trace_sems.at[window])
        for window in range(WINDOWS)
    ]
    whole_table.start()
    for copy in parts:
        copy.start()
    for copy in small:
        copy.start()
    for copy in small:
        copy.wait()
    lane = lax.broadcasted_iota(jnp.int32, (8, CHANNELS), 1)
    count_row = jnp.zeros((8, CHANNELS), jnp.int32)
    owner_row = jnp.zeros((8, CHANNELS), jnp.int32)
    mine = jnp.int32(0)
    found = jnp.int32(0)
    for step in range(SPAN):
        owner = owners[0, step]
        count_row = jnp.where(lane == step, counts[step, place[0]], count_row)
        owner_row = jnp.where(lane == step, owner, owner_row)
        here = owner == place[0]
        mine = jnp.where(here, step, mine)
        found = jnp.where(here, listed[0, step], found)
    total = jnp.int32(0)
    for group in range(GROUPS):
        total = total + counts[mine, group]
    weight[...] = jnp.full((8, LAGS), found, jnp.int32).astype(F32) / jnp.full(
        (8, LAGS), total, jnp.int32
    ).astype(F32)
    count_row = count_row.astype(F32)
    owner_row = owner_row.astype(F32)
    for part in range(BAND // 8):
        rows[pl.ds(part * 8 * CHUNK + 8, 8, stride=CHUNK), :] = count_row
        rows[pl.ds(part * 8 * CHUNK + 9, 8, stride=CHUNK), :] = owner_row
    whole_table.wait()
    for copy in parts:
        copy.wait()
    flat = traces[...].reshape(WINDOWS * CHANNELS, SAMPLES)
    both = lax.dot_general(
        table[...], flat, (((1,), (1,)), ((), ())), preferred_element_type=F32
    )
    spectrum = both[: 2 * BAND] + both[2 * BAND :]
    real_part = spectrum[:BAND]
    imag_part = spectrum[BAND:]
    amplitude = jnp.sqrt(real_part * real_part + imag_part * imag_part)
    near, everywhere = smooth_sums(amplitude)
    water_level = near / SMOOTH + WATER * (everywhere / BAND) + 1e-6
    real_part = real_part / water_level
    imag_part = imag_part / water_level
    for window in range(WINDOWS):
        here = slice(window * CHANNELS, (window + 1) * CHANNELS)
        rows[pl.ds(window, BAND, stride=CHUNK), :] = real_part[:, here]
        rows[pl.ds(WINDOWS + window, BAND, stride=CHUNK), :] = imag_part[:, here]
    out[...] = rows[...].astype(BF16)


def cross_kernel(
    chunks, to_high, to_low, back_high, back_low, out, rows, stacked, spectra, cross, slots
):
    rows[...] = chunks[...].astype(F32)
    block_rows = BLOCKS * CHUNK
    for group in range(PLANE_GROUPS):
        for window in range(WINDOWS):
            base = (group * WINDOWS + window) * BLOCKS
            for part in range(2):
                start = group * block_rows + part * WINDOWS + window
                lanes = slice(part * CHANNELS, (part + 1) * CHANNELS)
                stacked[base : base + BLOCKS, lanes] = rows[
                    pl.ds(start, BLOCKS, stride=CHUNK), :
                ]
    block_data = stacked[...].astype(BF16)
    both = dot(block_data, to_high[...]) + dot(block_data, to_low[...])
    for tile in range(4):
        lanes = slice(tile * 128, (tile + 1) * 128)
        for window in range(PLANE_GROUPS * WINDOWS):
            source, target = window * BLOCKS, window * EXTENDED
            spectra[tile, target : target + SPAN, :] = both[source + SPAN : source + BLOCKS, lanes]
            spectra[tile, target + SPAN : target + EXTENDED, :] = both[
                source : source + BLOCKS, lanes
            ]
    counts = [
        rows[pl.ds(group * block_rows + 8, 16, stride=CHUNK), :] for group in range(PLANE_GROUPS)
    ]
    owners = rows[pl.ds(9, 16, stride=CHUNK), :]
    for step in range(SPAN):
        distance = step + 1
        limits = [
            jnp.broadcast_to(counts[group][:, step : step + 1], (BLOCKS, 128))
            for group in range(PLANE_GROUPS)
        ]
        for half in range(2):
            total_real = jnp.zeros((BLOCKS, 128), F32)
            total_imag = jnp.zeros((BLOCKS, 128), F32)
            for group in range(PLANE_GROUPS):
                for window in range(WINDOWS):
                    base = (group * WINDOWS + window) * EXTENDED + SPAN
                    own = slice(base, base + BLOCKS)
                    before = slice(base - distance, base - distance + BLOCKS)
                    own_real = spectra[half, own, :]
                    own_imag = spectra[2 + half, own, :]
                    src_real = spectra[half, before, :]
                    src_imag = spectra[2 + half, before, :]
                    term_real = src_real * own_real + src_imag * own_imag
                    term_imag = src_real * own_imag - src_imag * own_real
                    if window > 0:
                        keep = limits[group] > float(window)
                        term_real = jnp.where(keep, term_real, 0.0)
                        term_imag = jnp.where(keep, term_imag, 0.0)
                    total_real = total_real + term_real
                    total_imag = total_imag + term_imag
            here = slice(step * BLOCKS, (step + 1) * BLOCKS)
            cross[here, half * 128 : (half + 1) * 128] = total_real
            cross[here, PADDED + half * 128 : PADDED + (half + 1) * 128] = total_imag
    partial = dot_split(cross[...], back_high[...], back_low[...])
    owner_of = [
        jnp.broadcast_to(owners[:, step : step + 1], (BLOCKS, 128)) for step in range(SPAN)
    ]
    for owner in range(GROUPS):
        halves = [jnp.zeros((BLOCKS, 128), F32), jnp.zeros((BLOCKS, 128), F32)]
        for step in range(SPAN):
            chosen = owner_of[step] == float(owner)
            for half in range(2):
                piece = partial[
                    step * BLOCKS : (step + 1) * BLOCKS, half * 128 : (half + 1) * 128
                ]
                halves[half] = jnp.where(chosen, piece, halves[half])
        for half in range(2):
            slots[pl.ds(owner * 2 * BLOCKS + half, BLOCKS, stride=2), :] = halves[half]
    out[...] = slots[...].astype(BF16)


def lag_kernel(arrived, weight, table_high, table_low, out):
    summed = arrived[: 2 * BAND].astype(F32)
    for layer in range(1, 8):
        summed = summed + arrived[layer * 2 * BAND : (layer + 1) * 2 * BAND].astype(F32)
    lagged = dot_split(summed.T, table_high[...], table_low[...])
    out[...] = lagged * weight[:1]


def shards(traces, pair_listed, owner_slot, window_count):
    vmem = pl.BlockSpec(memory_space=pltpu.VMEM)
    smem = pl.BlockSpec(memory_space=pltpu.SMEM)
    place = lax.axis_index(TM).astype(jnp.int32).reshape(1)
    hbm = pl.BlockSpec(memory_space=pltpu.HBM)
    chunks, weight = pl.pallas_call(
        whiten_kernel,
        out_shape=(
            jax.ShapeDtypeStruct((BAND * CHUNK, CHANNELS), BF16),
            jax.ShapeDtypeStruct((8, LAGS), F32),
        ),
        in_specs=[smem, hbm, hbm, hbm, hbm, hbm],
        out_specs=(vmem, vmem),
        scratch_shapes=[
            pltpu.SMEM((1, SPAN), jnp.int32),
            pltpu.SMEM((1, SPAN), jnp.int32),
            pltpu.SMEM((SPAN, GROUPS), jnp.int32),
            pltpu.VMEM((WINDOWS, CHANNELS, SAMPLES), BF16),
            pltpu.VMEM((4 * BAND, SAMPLES), BF16),
            pltpu.VMEM((BAND * CHUNK, CHANNELS), F32),
            pltpu.SemaphoreType.DMA((3,)),
            pltpu.SemaphoreType.DMA,
            pltpu.SemaphoreType.DMA((WINDOWS,)),
        ],
        compiler_params=pltpu.CompilerParams(vmem_limit_bytes=60 << 20),
        name="whiten",
    )(place, pair_listed, owner_slot, window_count[0], traces[0], band_table())
    chunks = chunks.reshape(BAND, CHUNK // 2, 2, CHANNELS)
    chunks = lax.all_to_all(chunks, PLANE, 0, 0, tiled=True)
    chunks = chunks.reshape(BAND * CHUNK, CHANNELS)
    slots = pl.pallas_call(
        cross_kernel,
        out_shape=jax.ShapeDtypeStruct((GROUPS * BLOCKS * 2, OFFSETS), BF16),
        in_specs=[vmem] * 5,
        out_specs=vmem,
        scratch_shapes=[
            pltpu.VMEM((BAND * CHUNK, CHANNELS), F32),
            pltpu.VMEM((PLANE_GROUPS * WINDOWS * BLOCKS, 2 * CHANNELS), F32),
            pltpu.VMEM((4, PLANE_GROUPS * WINDOWS * EXTENDED, 128), F32),
            pltpu.VMEM((SPAN * BLOCKS, 2 * PADDED), F32),
            pltpu.VMEM((GROUPS * BLOCKS * 2, OFFSETS), F32),
        ],
        compiler_params=pltpu.CompilerParams(vmem_limit_bytes=32 << 20),
        name="cross",
    )(chunks, *channel_table(), *offset_table())
    slots = slots.reshape(GROUPS * BLOCKS, 2, OFFSETS)
    slots = lax.all_to_all(slots, WHOLE, 0, 0, tiled=True)
    slots = slots.reshape(GROUPS * BLOCKS * 2, OFFSETS)
    stacked = pl.pallas_call(
        lag_kernel,
        out_shape=jax.ShapeDtypeStruct((OFFSETS, LAGS), F32),
        in_specs=[vmem] * 4,
        out_specs=vmem,
        compiler_params=pltpu.CompilerParams(vmem_limit_bytes=32 << 20),
        name="lag",
    )(slots, weight, *lag_table())
    return stacked[None, None]


def solution(mesh):
    fine = Mesh(mesh.devices.reshape(4, 2, 2, 8, 4), CHAN + TM)
    placed = (
        P(CHAN, TM, None, None),
        P(CHAN, None),
        P(CHAN, None),
        P(CHAN, None, None),
    )
    return jax.shard_map(
        shards, mesh=fine, in_specs=placed, out_specs=P(CHAN, TM, None, None), check_vma=False
    )
```

```python
import math

import jax
import jax.numpy as jnp
import ml_dtypes
import numpy as np
from jax import lax
from jax.experimental import pallas as pl
from jax.experimental.pallas import tpu as pltpu
from jax.sharding import Mesh
from jax.sharding import PartitionSpec as P

BAND = 64
SMOOTH = 16
OFFSETS = 128
LAGS = 128
WATER = 0.1
CHANNELS = 128
SAMPLES = 512
PADDED = 192
WINDOWS = 4
BLOCKS = 16
GROUPS = 32
SPAN = 8
PLANE_GROUPS = 4
CHUNK = 10
EXTENDED = BLOCKS + SPAN

CHAN = ("x", "yh", "core")
TM = ("z", "yl")
PLANE = ("yl",) + CHAN
WHOLE = TM + CHAN
F32 = jnp.float32
BF16 = jnp.bfloat16


def angles(left, right, period):
    return 2.0 * np.pi / period * ((left[:, None] * right[None, :]) % period)


def split_table(table):
    table = table.astype(np.float32)
    high = table.astype(ml_dtypes.bfloat16)
    low = (table - high.astype(np.float32)).astype(ml_dtypes.bfloat16)
    return high, low


def band_table():
    turn = angles(np.arange(BAND) + 1, np.arange(SAMPLES), SAMPLES)
    high, low = split_table(np.concatenate([np.cos(turn), -np.sin(turn)], axis=0))
    return np.concatenate([high, low], axis=0)


def channel_table():
    turn = angles(np.arange(CHANNELS), np.arange(PADDED), PADDED)
    real_part = np.concatenate([np.cos(turn), np.sin(turn)], axis=0)
    imag_part = np.concatenate([-np.sin(turn), np.cos(turn)], axis=0)
    real_rest, imag_rest = real_part[:, 128:], imag_part[:, 128:]
    return split_table(
        np.concatenate(
            [real_part[:, :128], imag_part[:, :128], real_rest, imag_rest, imag_rest, real_rest],
            axis=1,
        )
    )


def offset_table():
    turn = angles(np.arange(PADDED), np.arange(OFFSETS) - OFFSETS // 2, PADDED)
    of_real = np.concatenate([np.cos(turn), np.sin(turn)], axis=1) / PADDED
    of_imag = np.concatenate([-np.sin(turn), np.cos(turn)], axis=1) / PADDED
    real_rest, imag_rest = of_real[128:], of_imag[128:]
    return split_table(
        np.concatenate(
            [of_real[:128], of_imag[:128], real_rest, real_rest, imag_rest, -imag_rest], axis=0
        )
    )


def lag_table():
    turn = angles(np.arange(BAND) + 1, np.arange(LAGS) - LAGS // 2, SAMPLES)
    pair = np.stack([np.cos(turn), -np.sin(turn)], axis=1).reshape(2 * BAND, LAGS)
    return split_table(pair / math.sqrt(BAND))


def dot(left, right):
    return jnp.dot(left, right, preferred_element_type=F32)


def split(value):
    high = value.astype(BF16)
    return high, (value - high.astype(F32)).astype(BF16)


def dot_split(value, table_high, table_low):
    high, low = split(value)
    return dot(high, table_high) + (dot(low, table_high) + dot(high, table_low))


def smooth_sums(amplitude):
    target = lax.broadcasted_iota(jnp.int32, (2 * BAND, BAND), 0)
    source = lax.broadcasted_iota(jnp.int32, (2 * BAND, BAND), 1)
    start = jnp.clip(target - SMOOTH // 2, 0, BAND - SMOOTH)
    inside = (target >= BAND) | ((source >= start) & (source < start + SMOOTH))
    smooth = inside.astype(F32).astype(BF16)
    high, low = split(amplitude)
    sums = dot(smooth, high) + dot(smooth, low)
    return sums[:BAND], sums[BAND:]


def whiten_kernel(
    place,
    listed_hbm,
    owners_hbm,
    counts_hbm,
    traces_hbm,
    table_hbm,
    out,
    weight,
    listed,
    owners,
    counts,
    traces,
    table,
    rows,
    small_sems,
    table_sem,
    trace_sem,
):
    small = [
        pltpu.make_async_copy(source, target, small_sems.at[k])
        for k, (source, target) in enumerate(
            ((listed_hbm, listed), (owners_hbm, owners), (counts_hbm, counts))
        )
    ]
    whole_table = pltpu.make_async_copy(table_hbm, table, table_sem)
    whole_traces = pltpu.make_async_copy(traces_hbm, traces, trace_sem)
    whole_table.start()
    whole_traces.start()
    for copy in small:
        copy.start()
    for copy in small:
        copy.wait()
    lane = lax.broadcasted_iota(jnp.int32, (8, CHANNELS), 1)
    count_row = jnp.zeros((8, CHANNELS), jnp.int32)
    owner_row = jnp.zeros((8, CHANNELS), jnp.int32)
    mine = jnp.int32(0)
    found = jnp.int32(0)
    for step in range(SPAN):
        owner = owners[0, step]
        count_row = jnp.where(lane == step, counts[step, place[0]], count_row)
        owner_row = jnp.where(lane == step, owner, owner_row)
        here = owner == place[0]
        mine = jnp.where(here, step, mine)
        found = jnp.where(here, listed[0, step], found)
    total = jnp.int32(0)
    for group in range(GROUPS):
        total = total + counts[mine, group]
    weight[...] = jnp.full((8, LAGS), found, jnp.int32).astype(F32) / jnp.full(
        (8, LAGS), total, jnp.int32
    ).astype(F32)
    count_row = count_row.astype(F32)
    owner_row = owner_row.astype(F32)
    for part in range(BAND // 8):
        rows[pl.ds(part * 8 * CHUNK + 8, 8, stride=CHUNK), :] = count_row
        rows[pl.ds(part * 8 * CHUNK + 9, 8, stride=CHUNK), :] = owner_row
    whole_table.wait()
    whole_traces.wait()
    flat = traces[...].reshape(WINDOWS * CHANNELS, SAMPLES)
    both = lax.dot_general(
        table[...], flat, (((1,), (1,)), ((), ())), preferred_element_type=F32
    )
    spectrum = both[: 2 * BAND] + both[2 * BAND :]
    real_part = spectrum[:BAND]
    imag_part = spectrum[BAND:]
    amplitude = jnp.sqrt(real_part * real_part + imag_part * imag_part)
    near, everywhere = smooth_sums(amplitude)
    water_level = near / SMOOTH + WATER * (everywhere / BAND) + 1e-6
    real_part = real_part / water_level
    imag_part = imag_part / water_level
    for window in range(WINDOWS):
        here = slice(window * CHANNELS, (window + 1) * CHANNELS)
        rows[pl.ds(window, BAND, stride=CHUNK), :] = real_part[:, here]
        rows[pl.ds(WINDOWS + window, BAND, stride=CHUNK), :] = imag_part[:, here]
    out[...] = rows[...].astype(BF16)


def cross_kernel(
    chunks, to_high, to_low, back_high, back_low, out, rows, stacked, spectra, cross, pieces, named
):
    rows[...] = chunks[...].astype(F32)
    block_rows = BLOCKS * CHUNK
    for group in range(PLANE_GROUPS):
        for window in range(WINDOWS):
            base = (group * WINDOWS + window) * BLOCKS
            for part in range(2):
                start = group * block_rows + part * WINDOWS + window
                lanes = slice(part * CHANNELS, (part + 1) * CHANNELS)
                stacked[base : base + BLOCKS, lanes] = rows[
                    pl.ds(start, BLOCKS, stride=CHUNK), :
                ]
    block_data = stacked[...].astype(BF16)
    both = dot(block_data, to_high[...]) + dot(block_data, to_low[...])
    for tile in range(4):
        lanes = slice(tile * 128, (tile + 1) * 128)
        for window in range(PLANE_GROUPS * WINDOWS):
            source, target = window * BLOCKS, window * EXTENDED
            spectra[tile, target : target + SPAN, :] = both[source + SPAN : source + BLOCKS, lanes]
            spectra[tile, target + SPAN : target + EXTENDED, :] = both[
                source : source + BLOCKS, lanes
            ]
    counts = [
        rows[pl.ds(group * block_rows + 8, 16, stride=CHUNK), :] for group in range(PLANE_GROUPS)
    ]
    owners = rows[pl.ds(9, 16, stride=CHUNK), :]
    for step in range(SPAN):
        distance = step + 1
        limits = [
            jnp.broadcast_to(counts[group][:, step : step + 1], (BLOCKS, 128))
            for group in range(PLANE_GROUPS)
        ]
        here = slice(step * BLOCKS, (step + 1) * BLOCKS)
        for half in range(2):
            first = jnp.zeros((BLOCKS, 128), F32)
            second = jnp.zeros((BLOCKS, 128), F32)
            for group in range(PLANE_GROUPS):
                for window in range(WINDOWS):
                    base = (group * WINDOWS + window) * EXTENDED + SPAN
                    own = slice(base, base + BLOCKS)
                    before = slice(base - distance, base - distance + BLOCKS)
                    if half == 0:
                        own_real = spectra[0, own, :]
                        own_imag = spectra[1, own, :]
                        src_real = spectra[0, before, :]
                        src_imag = spectra[1, before, :]
                        term_first = src_real * own_real + src_imag * own_imag
                        term_second = src_real * own_imag - src_imag * own_real
                    else:
                        source = spectra[2, before, :]
                        term_first = source * spectra[2, own, :]
                        term_second = source * spectra[3, own, :]
                    if window > 0:
                        keep = limits[group] > float(window)
                        term_first = jnp.where(keep, term_first, 0.0)
                        term_second = jnp.where(keep, term_second, 0.0)
                    first = first + term_first
                    second = second + term_second
            cross[here, half * 256 : half * 256 + 128] = first
            cross[here, half * 256 + 128 : half * 256 + 256] = second
        chosen = jnp.broadcast_to(owners[:, step : step + 1], (BLOCKS, 128))
        for half in range(2):
            named[pl.ds(step * 2 * BLOCKS + half, BLOCKS, stride=2), :] = chosen
    high, low = split(cross[...])
    pairs = SPAN * BLOCKS
    by_high = dot(jnp.concatenate([high, low], axis=0), back_high[...])
    partial = by_high[:pairs] + (by_high[pairs:] + dot(high, back_low[...]))
    for half in range(2):
        pieces[pl.ds(half, pairs, stride=2), :] = partial[:, half * 128 : (half + 1) * 128]
    lines = 2 * BLOCKS
    piece_of = [
        pieces[step * lines : (step + 1) * lines, :].astype(BF16) for step in range(SPAN)
    ]
    owner_of = [
        named[step * lines : (step + 1) * lines, :].astype(BF16) for step in range(SPAN)
    ]
    for owner in range(GROUPS):
        chunk = jnp.zeros((lines, OFFSETS), BF16)
        for step in range(SPAN):
            chunk = jnp.where(owner_of[step] == jnp.bfloat16(owner), piece_of[step], chunk)
        out[owner * lines : (owner + 1) * lines, :] = chunk


def lag_kernel(arrived, weight, table_high, table_low, out):
    summed = arrived[: 2 * BAND].astype(F32)
    for layer in range(1, 8):
        summed = summed + arrived[layer * 2 * BAND : (layer + 1) * 2 * BAND].astype(F32)
    lagged = dot_split(summed.T, table_high[...], table_low[...])
    out[...] = lagged * weight[:1]


def shards(traces, pair_listed, owner_slot, window_count):
    vmem = pl.BlockSpec(memory_space=pltpu.VMEM)
    smem = pl.BlockSpec(memory_space=pltpu.SMEM)
    place = lax.axis_index(TM).astype(jnp.int32).reshape(1)
    hbm = pl.BlockSpec(memory_space=pltpu.HBM)
    chunks, weight = pl.pallas_call(
        whiten_kernel,
        out_shape=(
            jax.ShapeDtypeStruct((BAND * CHUNK, CHANNELS), BF16),
            jax.ShapeDtypeStruct((8, LAGS), F32),
        ),
        in_specs=[smem, hbm, hbm, hbm, hbm, hbm],
        out_specs=(vmem, vmem),
        scratch_shapes=[
            pltpu.SMEM((1, SPAN), jnp.int32),
            pltpu.SMEM((1, SPAN), jnp.int32),
            pltpu.SMEM((SPAN, GROUPS), jnp.int32),
            pltpu.VMEM((WINDOWS, CHANNELS, SAMPLES), BF16),
            pltpu.VMEM((4 * BAND, SAMPLES), BF16),
            pltpu.VMEM((BAND * CHUNK, CHANNELS), F32),
            pltpu.SemaphoreType.DMA((3,)),
            pltpu.SemaphoreType.DMA,
            pltpu.SemaphoreType.DMA,
        ],
        compiler_params=pltpu.CompilerParams(vmem_limit_bytes=32 << 20),
        name="whiten",
    )(
        place,
        *(
            pltpu.with_memory_space_constraint(operand, pltpu.HBM)
            for operand in (pair_listed, owner_slot, window_count[0], traces[0], band_table())
        ),
    )
    chunks = chunks.reshape(BAND, CHUNK // 2, 2, CHANNELS)
    chunks = lax.all_to_all(chunks, PLANE, 0, 0, tiled=True)
    chunks = chunks.reshape(BAND * CHUNK, CHANNELS)
    slots = pl.pallas_call(
        cross_kernel,
        out_shape=jax.ShapeDtypeStruct((GROUPS * BLOCKS * 2, OFFSETS), BF16),
        in_specs=[vmem] * 5,
        out_specs=vmem,
        scratch_shapes=[
            pltpu.VMEM((BAND * CHUNK, CHANNELS), F32),
            pltpu.VMEM((PLANE_GROUPS * WINDOWS * BLOCKS, 2 * CHANNELS), F32),
            pltpu.VMEM((4, PLANE_GROUPS * WINDOWS * EXTENDED, 128), F32),
            pltpu.VMEM((SPAN * BLOCKS, 512), F32),
            pltpu.VMEM((SPAN * BLOCKS * 2, OFFSETS), F32),
            pltpu.VMEM((SPAN * BLOCKS * 2, OFFSETS), F32),
        ],
        compiler_params=pltpu.CompilerParams(vmem_limit_bytes=32 << 20),
        name="cross",
    )(chunks, *channel_table(), *offset_table())
    slots = slots.reshape(GROUPS * BLOCKS, 2, OFFSETS)
    slots = lax.all_to_all(slots, WHOLE, 0, 0, tiled=True)
    slots = slots.reshape(GROUPS * BLOCKS * 2, OFFSETS)
    stacked = pl.pallas_call(
        lag_kernel,
        out_shape=jax.ShapeDtypeStruct((OFFSETS, LAGS), F32),
        in_specs=[vmem] * 4,
        out_specs=vmem,
        compiler_params=pltpu.CompilerParams(vmem_limit_bytes=32 << 20),
        name="lag",
    )(slots, weight, *lag_table())
    return stacked[None, None]


def solution(mesh):
    fine = Mesh(mesh.devices.reshape(4, 2, 2, 8, 4), CHAN + TM)
    placed = (
        P(CHAN, TM, None, None),
        P(CHAN, None),
        P(CHAN, None),
        P(CHAN, None, None),
    )
    return jax.shard_map(
        shards, mesh=fine, in_specs=placed, out_specs=P(CHAN, TM, None, None), check_vma=False
    )
```

```python
import math

import jax
import jax.numpy as jnp
import ml_dtypes
import numpy as np
from jax import lax
from jax.experimental import pallas as pl
from jax.experimental.pallas import tpu as pltpu
from jax.sharding import Mesh
from jax.sharding import PartitionSpec as P

BAND = 64
SMOOTH = 16
OFFSETS = 128
LAGS = 128
WATER = 0.1
CHANNELS = 128
SAMPLES = 512
PADDED = 192
WINDOWS = 4
BLOCKS = 16
GROUPS = 32
SPAN = 8
PLANE_GROUPS = 4
CHUNK = 10
EXTENDED = BLOCKS + SPAN

CHAN = ("x", "yh", "core")
TM = ("z", "yl")
PLANE = ("yl",) + CHAN
WHOLE = TM + CHAN
F32 = jnp.float32
BF16 = jnp.bfloat16


def angles(left, right, period):
    return 2.0 * np.pi / period * ((left[:, None] * right[None, :]) % period)


def split_table(table):
    table = table.astype(np.float32)
    high = table.astype(ml_dtypes.bfloat16)
    low = (table - high.astype(np.float32)).astype(ml_dtypes.bfloat16)
    return high, low


def band_table():
    turn = angles(np.arange(BAND) + 1, np.arange(SAMPLES), SAMPLES)
    high, low = split_table(np.concatenate([np.cos(turn), -np.sin(turn)], axis=0))
    return np.concatenate([high, low], axis=0)


def channel_table():
    turn = angles(np.arange(CHANNELS), np.arange(PADDED), PADDED)
    real_part = np.concatenate([np.cos(turn), np.sin(turn)], axis=0)
    imag_part = np.concatenate([-np.sin(turn), np.cos(turn)], axis=0)
    real_rest, imag_rest = real_part[:, 128:], imag_part[:, 128:]
    return split_table(
        np.concatenate(
            [real_part[:, :128], imag_part[:, :128], real_rest, imag_rest, imag_rest, real_rest],
            axis=1,
        )
    )


def offset_table():
    turn = angles(np.arange(PADDED), np.arange(OFFSETS) - OFFSETS // 2, PADDED)
    of_real = np.concatenate([np.cos(turn), np.sin(turn)], axis=1) / PADDED
    of_imag = np.concatenate([-np.sin(turn), np.cos(turn)], axis=1) / PADDED
    real_rest, imag_rest = of_real[128:], of_imag[128:]
    return split_table(
        np.concatenate(
            [of_real[:128], of_imag[:128], real_rest, real_rest, imag_rest, -imag_rest], axis=0
        )
    )


def lag_table():
    turn = angles(np.arange(BAND) + 1, np.arange(LAGS) - LAGS // 2, SAMPLES)
    pair = np.stack([np.cos(turn), -np.sin(turn)], axis=1).reshape(2 * BAND, LAGS)
    return split_table(pair / math.sqrt(BAND))


def dot(left, right):
    return jnp.dot(left, right, preferred_element_type=F32)


def split(value):
    high = value.astype(BF16)
    return high, (value - high.astype(F32)).astype(BF16)


def dot_split(value, table_high, table_low):
    high, low = split(value)
    return dot(high, table_high) + (dot(low, table_high) + dot(high, table_low))


def smooth_sums(amplitude):
    target = lax.broadcasted_iota(jnp.int32, (2 * BAND, BAND), 0)
    source = lax.broadcasted_iota(jnp.int32, (2 * BAND, BAND), 1)
    start = jnp.clip(target - SMOOTH // 2, 0, BAND - SMOOTH)
    inside = (target >= BAND) | ((source >= start) & (source < start + SMOOTH))
    smooth = inside.astype(F32).astype(BF16)
    high, low = split(amplitude)
    sums = dot(smooth, high) + dot(smooth, low)
    return sums[:BAND], sums[BAND:]


def whiten_kernel(
    place,
    listed_hbm,
    owners_hbm,
    counts_hbm,
    traces_hbm,
    table_hbm,
    out,
    weight,
    listed,
    owners,
    counts,
    traces,
    table,
    rows,
    small_sems,
    table_sem,
    trace_sem,
):
    small = [
        pltpu.make_async_copy(source, target, small_sems.at[k])
        for k, (source, target) in enumerate(
            ((listed_hbm, listed), (owners_hbm, owners), (counts_hbm, counts))
        )
    ]
    whole_table = pltpu.make_async_copy(table_hbm, table, table_sem)
    whole_traces = pltpu.make_async_copy(traces_hbm, traces, trace_sem)
    whole_table.start()
    whole_traces.start()
    for copy in small:
        copy.start()
    for copy in small:
        copy.wait()
    lane = lax.broadcasted_iota(jnp.int32, (8, CHANNELS), 1)
    count_row = jnp.zeros((8, CHANNELS), jnp.int32)
    owner_row = jnp.zeros((8, CHANNELS), jnp.int32)
    mine = jnp.int32(0)
    found = jnp.int32(0)
    for step in range(SPAN):
        owner = owners[0, step]
        count_row = jnp.where(lane == step, counts[step, place[0]], count_row)
        owner_row = jnp.where(lane == step, owner, owner_row)
        here = owner == place[0]
        mine = jnp.where(here, step, mine)
        found = jnp.where(here, listed[0, step], found)
    total = jnp.int32(0)
    for group in range(GROUPS):
        total = total + counts[mine, group]
    weight[...] = jnp.full((8, LAGS), found, jnp.int32).astype(F32) / jnp.full(
        (8, LAGS), total, jnp.int32
    ).astype(F32)
    count_row = count_row.astype(F32)
    owner_row = owner_row.astype(F32)
    for part in range(BAND // 8):
        rows[pl.ds(part * 8 * CHUNK + 8, 8, stride=CHUNK), :] = count_row
        rows[pl.ds(part * 8 * CHUNK + 9, 8, stride=CHUNK), :] = owner_row
    whole_table.wait()
    whole_traces.wait()
    flat = traces[...].reshape(WINDOWS * CHANNELS, SAMPLES)
    both = lax.dot_general(
        table[...], flat, (((1,), (1,)), ((), ())), preferred_element_type=F32
    )
    spectrum = both[: 2 * BAND] + both[2 * BAND :]
    real_part = spectrum[:BAND]
    imag_part = spectrum[BAND:]
    amplitude = jnp.sqrt(real_part * real_part + imag_part * imag_part)
    near, everywhere = smooth_sums(amplitude)
    water_level = near / SMOOTH + WATER * (everywhere / BAND) + 1e-6
    real_part = real_part / water_level
    imag_part = imag_part / water_level
    for window in range(WINDOWS):
        here = slice(window * CHANNELS, (window + 1) * CHANNELS)
        rows[pl.ds(window, BAND, stride=CHUNK), :] = real_part[:, here]
        rows[pl.ds(WINDOWS + window, BAND, stride=CHUNK), :] = imag_part[:, here]
    out[...] = rows[...].astype(BF16)


def cross_kernel(
    chunks, to_high, to_low, back_high, back_low, out, rows, spectra, cross, pieces, named
):
    rows[...] = chunks[...].astype(F32)
    block_rows = BLOCKS * CHUNK
    block_data = jnp.concatenate(
        [
            jnp.concatenate(
                [
                    rows[pl.ds(group * block_rows + part * WINDOWS + window, BLOCKS, stride=CHUNK), :]
                    for part in range(2)
                ],
                axis=1,
            ).astype(BF16)
            for group in range(PLANE_GROUPS)
            for window in range(WINDOWS)
        ],
        axis=0,
    )
    both = dot(block_data, to_high[...]) + dot(block_data, to_low[...])
    for tile in range(4):
        lanes = slice(tile * 128, (tile + 1) * 128)
        for window in range(PLANE_GROUPS * WINDOWS):
            source, target = window * BLOCKS, window * EXTENDED
            spectra[tile, target : target + SPAN, :] = both[source + SPAN : source + BLOCKS, lanes]
            spectra[tile, target + SPAN : target + EXTENDED, :] = both[
                source : source + BLOCKS, lanes
            ]
    counts = [
        rows[pl.ds(group * block_rows + 8, 16, stride=CHUNK), :] for group in range(PLANE_GROUPS)
    ]
    owners = rows[pl.ds(9, 16, stride=CHUNK), :]
    for step in range(SPAN):
        distance = step + 1
        limits = [
            jnp.broadcast_to(counts[group][:, step : step + 1], (BLOCKS, 128))
            for group in range(PLANE_GROUPS)
        ]
        here = slice(step * BLOCKS, (step + 1) * BLOCKS)
        for half in range(2):
            first = jnp.zeros((BLOCKS, 128), F32)
            second = jnp.zeros((BLOCKS, 128), F32)
            for group in range(PLANE_GROUPS):
                for window in range(WINDOWS):
                    base = (group * WINDOWS + window) * EXTENDED + SPAN
                    own = slice(base, base + BLOCKS)
                    before = slice(base - distance, base - distance + BLOCKS)
                    keep = limits[group] > float(window)
                    if half == 0:
                        own_real = spectra[0, own, :]
                        own_imag = spectra[1, own, :]
                        src_real = spectra[0, before, :]
                        src_imag = spectra[1, before, :]
                        if window > 0:
                            src_real = jnp.where(keep, src_real, 0.0)
                            src_imag = jnp.where(keep, src_imag, 0.0)
                        first = first + (src_real * own_real + src_imag * own_imag)
                        second = second + (src_real * own_imag - src_imag * own_real)
                    else:
                        source = spectra[2, before, :]
                        if window > 0:
                            source = jnp.where(keep, source, 0.0)
                        first = first + source * spectra[2, own, :]
                        second = second + source * spectra[3, own, :]
            cross[here, half * 256 : half * 256 + 128] = first
            cross[here, half * 256 + 128 : half * 256 + 256] = second
        chosen = jnp.broadcast_to(owners[:, step : step + 1], (BLOCKS, 128))
        for half in range(2):
            named[pl.ds(step * 2 * BLOCKS + half, BLOCKS, stride=2), :] = chosen
    high, low = split(cross[...])
    pairs = SPAN * BLOCKS
    by_high = dot(jnp.concatenate([high, low], axis=0), back_high[...])
    partial = by_high[:pairs] + (by_high[pairs:] + dot(high, back_low[...]))
    for half in range(2):
        pieces[pl.ds(half, pairs, stride=2), :] = partial[:, half * 128 : (half + 1) * 128]
    lines = 2 * BLOCKS
    piece_of = [
        pieces[step * lines : (step + 1) * lines, :].astype(BF16) for step in range(SPAN)
    ]
    owner_of = [
        named[step * lines : (step + 1) * lines, :].astype(BF16) for step in range(SPAN)
    ]
    for owner in range(GROUPS):
        chunk = jnp.zeros((lines, OFFSETS), BF16)
        for step in range(SPAN):
            chunk = jnp.where(owner_of[step] == jnp.bfloat16(owner), piece_of[step], chunk)
        out[owner * lines : (owner + 1) * lines, :] = chunk


def lag_kernel(arrived, weight, table_high, table_low, out):
    summed = arrived[: 2 * BAND].astype(F32)
    for layer in range(1, 8):
        summed = summed + arrived[layer * 2 * BAND : (layer + 1) * 2 * BAND].astype(F32)
    lagged = dot_split(summed.T, table_high[...], table_low[...])
    out[...] = lagged * weight[:1]


def shards(traces, pair_listed, owner_slot, window_count):
    vmem = pl.BlockSpec(memory_space=pltpu.VMEM)
    smem = pl.BlockSpec(memory_space=pltpu.SMEM)
    place = lax.axis_index(TM).astype(jnp.int32).reshape(1)
    hbm = pl.BlockSpec(memory_space=pltpu.HBM)
    chunks, weight = pl.pallas_call(
        whiten_kernel,
        out_shape=(
            jax.ShapeDtypeStruct((BAND * CHUNK, CHANNELS), BF16),
            jax.ShapeDtypeStruct((8, LAGS), F32),
        ),
        in_specs=[smem, hbm, hbm, hbm, hbm, hbm],
        out_specs=(vmem, vmem),
        scratch_shapes=[
            pltpu.SMEM((1, SPAN), jnp.int32),
            pltpu.SMEM((1, SPAN), jnp.int32),
            pltpu.SMEM((SPAN, GROUPS), jnp.int32),
            pltpu.VMEM((WINDOWS, CHANNELS, SAMPLES), BF16),
            pltpu.VMEM((4 * BAND, SAMPLES), BF16),
            pltpu.VMEM((BAND * CHUNK, CHANNELS), F32),
            pltpu.SemaphoreType.DMA((3,)),
            pltpu.SemaphoreType.DMA,
            pltpu.SemaphoreType.DMA,
        ],
        compiler_params=pltpu.CompilerParams(vmem_limit_bytes=32 << 20),
        name="whiten",
    )(
        place,
        *(
            pltpu.with_memory_space_constraint(operand, pltpu.HBM)
            for operand in (pair_listed, owner_slot, window_count[0], traces[0], band_table())
        ),
    )
    chunks = chunks.reshape(BAND, CHUNK // 2, 2, CHANNELS)
    chunks = lax.all_to_all(chunks, PLANE, 0, 0, tiled=True)
    chunks = chunks.reshape(BAND * CHUNK, CHANNELS)
    slots = pl.pallas_call(
        cross_kernel,
        out_shape=jax.ShapeDtypeStruct((GROUPS * BLOCKS * 2, OFFSETS), BF16),
        in_specs=[vmem] * 5,
        out_specs=vmem,
        scratch_shapes=[
            pltpu.VMEM((BAND * CHUNK, CHANNELS), F32),
            pltpu.VMEM((4, PLANE_GROUPS * WINDOWS * EXTENDED, 128), F32),
            pltpu.VMEM((SPAN * BLOCKS, 512), F32),
            pltpu.VMEM((SPAN * BLOCKS * 2, OFFSETS), F32),
            pltpu.VMEM((SPAN * BLOCKS * 2, OFFSETS), F32),
        ],
        compiler_params=pltpu.CompilerParams(vmem_limit_bytes=32 << 20),
        name="cross",
    )(chunks, *channel_table(), *offset_table())
    slots = slots.reshape(GROUPS * BLOCKS, 2, OFFSETS)
    slots = lax.all_to_all(slots, WHOLE, 0, 0, tiled=True)
    slots = slots.reshape(GROUPS * BLOCKS * 2, OFFSETS)
    stacked = pl.pallas_call(
        lag_kernel,
        out_shape=jax.ShapeDtypeStruct((OFFSETS, LAGS), F32),
        in_specs=[vmem] * 4,
        out_specs=vmem,
        compiler_params=pltpu.CompilerParams(vmem_limit_bytes=32 << 20),
        name="lag",
    )(slots, weight, *lag_table())
    return stacked[None, None]


def solution(mesh):
    fine = Mesh(mesh.devices.reshape(4, 2, 2, 8, 4), CHAN + TM)
    placed = (
        P(CHAN, TM, None, None),
        P(CHAN, None),
        P(CHAN, None),
        P(CHAN, None, None),
    )
    return jax.shard_map(
        shards, mesh=fine, in_specs=placed, out_specs=P(CHAN, TM, None, None), check_vma=False
    )
```

```python
import math

import jax
import jax.numpy as jnp
import ml_dtypes
import numpy as np
from jax import lax
from jax.experimental import pallas as pl
from jax.experimental.pallas import tpu as pltpu
from jax.sharding import Mesh
from jax.sharding import PartitionSpec as P

BAND = 64
SMOOTH = 16
OFFSETS = 128
LAGS = 128
WATER = 0.1
CHANNELS = 128
SAMPLES = 512
PADDED = 192
WINDOWS = 4
BLOCKS = 16
GROUPS = 32
SPAN = 8
PLANE_GROUPS = 4
CHUNK = 10
EXTENDED = BLOCKS + SPAN

CHAN = ("x", "yh", "core")
TM = ("z", "yl")
PLANE = ("yl",) + CHAN
WHOLE = ("yl", "z", "core", "yh", "x")
DEPTH = GROUPS // PLANE_GROUPS
F32 = jnp.float32
BF16 = jnp.bfloat16


def angles(left, right, period):
    return 2.0 * np.pi / period * ((left[:, None] * right[None, :]) % period)


def split_table(table):
    table = table.astype(np.float32)
    high = table.astype(ml_dtypes.bfloat16)
    low = (table - high.astype(np.float32)).astype(ml_dtypes.bfloat16)
    return high, low


def band_table():
    turn = angles(np.arange(BAND) + 1, np.arange(SAMPLES), SAMPLES)
    high, low = split_table(np.concatenate([np.cos(turn), -np.sin(turn)], axis=0))
    return np.concatenate([high, low], axis=0)


def channel_table():
    turn = angles(np.arange(CHANNELS), np.arange(PADDED), PADDED)
    real_part = np.concatenate([np.cos(turn), np.sin(turn)], axis=0)
    imag_part = np.concatenate([-np.sin(turn), np.cos(turn)], axis=0)
    real_rest, imag_rest = real_part[:, 128:], imag_part[:, 128:]
    return split_table(
        np.concatenate(
            [real_part[:, :128], imag_part[:, :128], real_rest, imag_rest, imag_rest, real_rest],
            axis=1,
        )
    )


def offset_table():
    turn = angles(np.arange(PADDED), np.arange(OFFSETS) - OFFSETS // 2, PADDED)
    of_real = np.concatenate([np.cos(turn), np.sin(turn)], axis=1) / PADDED
    of_imag = np.concatenate([-np.sin(turn), np.cos(turn)], axis=1) / PADDED
    real_rest, imag_rest = of_real[128:], of_imag[128:]
    return split_table(
        np.concatenate(
            [of_real[:128], of_imag[:128], real_rest, real_rest, imag_rest, -imag_rest], axis=0
        )
    )


def block_order():
    return np.arange(BLOCKS).reshape(4, 2, 2).transpose(2, 1, 0).reshape(-1)


def order_table():
    pairs = SPAN * BLOCKS
    step, block, half = np.meshgrid(np.arange(SPAN), block_order(), np.arange(2), indexing="ij")
    source = (half * pairs + step * BLOCKS + block).reshape(-1)
    return (source[:, None] == np.arange(2 * pairs)[None, :]).astype(ml_dtypes.bfloat16)


def lag_table():
    bins = (np.arange(PLANE_GROUPS)[:, None] * BLOCKS + block_order()[None, :]).reshape(-1) + 1
    turn = angles(bins, np.arange(LAGS) - LAGS // 2, SAMPLES)
    pair = np.stack([np.cos(turn), -np.sin(turn)], axis=1).reshape(2 * BAND, LAGS)
    return split_table(pair / math.sqrt(BAND))


def dot(left, right):
    return jnp.dot(left, right, preferred_element_type=F32)


def split(value):
    high = value.astype(BF16)
    return high, (value - high.astype(F32)).astype(BF16)


def dot_split(value, table_high, table_low):
    high, low = split(value)
    return dot(high, table_high) + (dot(low, table_high) + dot(high, table_low))


def smooth_sums(amplitude):
    target = lax.broadcasted_iota(jnp.int32, (2 * BAND, BAND), 0)
    source = lax.broadcasted_iota(jnp.int32, (2 * BAND, BAND), 1)
    start = jnp.clip(target - SMOOTH // 2, 0, BAND - SMOOTH)
    inside = (target >= BAND) | ((source >= start) & (source < start + SMOOTH))
    smooth = inside.astype(F32).astype(BF16)
    high, low = split(amplitude)
    sums = dot(smooth, high) + dot(smooth, low)
    return sums[:BAND], sums[BAND:]


def whiten_kernel(
    place,
    listed_hbm,
    owners_hbm,
    counts_hbm,
    traces_hbm,
    table_hbm,
    out,
    weight,
    listed,
    owners,
    counts,
    traces,
    table,
    rows,
    small_sems,
    table_sem,
    trace_sem,
):
    small = [
        pltpu.make_async_copy(source, target, small_sems.at[k])
        for k, (source, target) in enumerate(
            ((listed_hbm, listed), (owners_hbm, owners), (counts_hbm, counts))
        )
    ]
    whole_table = pltpu.make_async_copy(table_hbm, table, table_sem)
    whole_traces = pltpu.make_async_copy(traces_hbm, traces, trace_sem)
    whole_table.start()
    whole_traces.start()
    for copy in small:
        copy.start()
    for copy in small:
        copy.wait()
    lane = lax.broadcasted_iota(jnp.int32, (8, CHANNELS), 1)
    count_row = jnp.zeros((8, CHANNELS), jnp.int32)
    owner_row = jnp.zeros((8, CHANNELS), jnp.int32)
    mine = jnp.int32(0)
    found = jnp.int32(0)
    for step in range(SPAN):
        owner = owners[0, step]
        count_row = jnp.where(lane == step, counts[step, place[0]], count_row)
        owner_row = jnp.where(lane == step, owner, owner_row)
        here = owner == place[0]
        mine = jnp.where(here, step, mine)
        found = jnp.where(here, listed[0, step], found)
    total = jnp.int32(0)
    for group in range(GROUPS):
        total = total + counts[mine, group]
    weight[...] = jnp.full((8, LAGS), found, jnp.int32).astype(F32) / jnp.full(
        (8, LAGS), total, jnp.int32
    ).astype(F32)
    count_row = count_row.astype(F32)
    owner_row = owner_row.astype(F32)
    for part in range(BAND // 8):
        rows[pl.ds(part * 8 * CHUNK + 8, 8, stride=CHUNK), :] = count_row
        rows[pl.ds(part * 8 * CHUNK + 9, 8, stride=CHUNK), :] = owner_row
    whole_table.wait()
    whole_traces.wait()
    flat = traces[...].reshape(WINDOWS * CHANNELS, SAMPLES)
    both = lax.dot_general(
        table[...], flat, (((1,), (1,)), ((), ())), preferred_element_type=F32
    )
    spectrum = both[: 2 * BAND] + both[2 * BAND :]
    real_part = spectrum[:BAND]
    imag_part = spectrum[BAND:]
    amplitude = jnp.sqrt(real_part * real_part + imag_part * imag_part)
    near, everywhere = smooth_sums(amplitude)
    water_level = near / SMOOTH + WATER * (everywhere / BAND) + 1e-6
    real_part = real_part / water_level
    imag_part = imag_part / water_level
    for window in range(WINDOWS):
        here = slice(window * CHANNELS, (window + 1) * CHANNELS)
        rows[pl.ds(window, BAND, stride=CHUNK), :] = real_part[:, here]
        rows[pl.ds(WINDOWS + window, BAND, stride=CHUNK), :] = imag_part[:, here]
    out[...] = rows[...].astype(BF16)


def cross_kernel(
    chunks, to_high, to_low, back_high, back_low, order, out, rows, spectra, cross
):
    rows[...] = chunks[...].astype(F32)
    block_rows = BLOCKS * CHUNK
    block_data = jnp.concatenate(
        [
            jnp.concatenate(
                [
                    rows[pl.ds(group * block_rows + part * WINDOWS + window, BLOCKS, stride=CHUNK), :]
                    for part in range(2)
                ],
                axis=1,
            ).astype(BF16)
            for group in range(PLANE_GROUPS)
            for window in range(WINDOWS)
        ],
        axis=0,
    )
    both = dot(block_data, to_high[...]) + dot(block_data, to_low[...])
    for tile in range(4):
        lanes = slice(tile * 128, (tile + 1) * 128)
        for window in range(PLANE_GROUPS * WINDOWS):
            source, target = window * BLOCKS, window * EXTENDED
            spectra[tile, target : target + SPAN, :] = both[source + SPAN : source + BLOCKS, lanes]
            spectra[tile, target + SPAN : target + EXTENDED, :] = both[
                source : source + BLOCKS, lanes
            ]
    counts = [
        rows[pl.ds(group * block_rows + 8, 16, stride=CHUNK), :] for group in range(PLANE_GROUPS)
    ]
    owners = rows[pl.ds(9, 16, stride=CHUNK), :]
    for step in range(SPAN):
        distance = step + 1
        limits = [
            jnp.broadcast_to(counts[group][:, step : step + 1], (BLOCKS, 128))
            for group in range(PLANE_GROUPS)
        ]
        here = slice(step * BLOCKS, (step + 1) * BLOCKS)
        for half in range(2):
            first = jnp.zeros((BLOCKS, 128), F32)
            second = jnp.zeros((BLOCKS, 128), F32)
            for group in range(PLANE_GROUPS):
                for window in range(WINDOWS):
                    base = (group * WINDOWS + window) * EXTENDED + SPAN
                    own = slice(base, base + BLOCKS)
                    before = slice(base - distance, base - distance + BLOCKS)
                    keep = limits[group] > float(window)
                    if half == 0:
                        own_real = spectra[0, own, :]
                        own_imag = spectra[1, own, :]
                        src_real = spectra[0, before, :]
                        src_imag = spectra[1, before, :]
                        if window > 0:
                            src_real = jnp.where(keep, src_real, 0.0)
                            src_imag = jnp.where(keep, src_imag, 0.0)
                        first = first + (src_real * own_real + src_imag * own_imag)
                        second = second + (src_real * own_imag - src_imag * own_real)
                    else:
                        source = spectra[2, before, :]
                        if window > 0:
                            source = jnp.where(keep, source, 0.0)
                        first = first + source * spectra[2, own, :]
                        second = second + source * spectra[3, own, :]
            cross[here, half * 256 : half * 256 + 128] = first
            cross[here, half * 256 + 128 : half * 256 + 256] = second
    high, low = split(cross[...])
    pairs = SPAN * BLOCKS
    by_high = dot(jnp.concatenate([high, low], axis=0), back_high[...])
    partial = by_high[:pairs] + (by_high[pairs:] + dot(high, back_low[...]))
    named = jnp.concatenate(
        [
            jnp.broadcast_to(owners[:, step : step + 1], (BLOCKS, OFFSETS))
            for step in range(SPAN)
        ],
        axis=0,
    )
    beside = jnp.concatenate(
        [
            jnp.concatenate([partial[:, :OFFSETS], named], axis=1),
            jnp.concatenate([partial[:, OFFSETS:], named], axis=1),
        ],
        axis=0,
    )
    ordered = dot(order[...], beside.astype(BF16)).astype(BF16)
    lines = 2 * BLOCKS
    for slot in range(GROUPS):
        owner = slot % DEPTH * PLANE_GROUPS + slot // DEPTH
        chunk = jnp.zeros((lines, OFFSETS), BF16)
        for step in range(SPAN):
            here = slice(step * lines, (step + 1) * lines)
            chosen = ordered[here, OFFSETS:] == jnp.bfloat16(owner)
            chunk = jnp.where(chosen, ordered[here, :OFFSETS], chunk)
        out[slot * lines : (slot + 1) * lines, :] = chunk


def lag_kernel(arrived, weight, table_high, table_low, out):
    lines = 2 * BLOCKS
    sums = []
    for group in range(PLANE_GROUPS):
        first = group * DEPTH * lines
        total = arrived[first : first + lines].astype(F32)
        for layer in range(1, DEPTH):
            start = first + layer * lines
            total = total + arrived[start : start + lines].astype(F32)
        sums.append(total)
    summed = jnp.concatenate(sums, axis=0)
    lagged = dot_split(summed.T, table_high[...], table_low[...])
    out[...] = lagged * weight[:1]


def shards(traces, pair_listed, owner_slot, window_count):
    vmem = pl.BlockSpec(memory_space=pltpu.VMEM)
    smem = pl.BlockSpec(memory_space=pltpu.SMEM)
    place = lax.axis_index(TM).astype(jnp.int32).reshape(1)
    hbm = pl.BlockSpec(memory_space=pltpu.HBM)
    chunks, weight = pl.pallas_call(
        whiten_kernel,
        out_shape=(
            jax.ShapeDtypeStruct((BAND * CHUNK, CHANNELS), BF16),
            jax.ShapeDtypeStruct((8, LAGS), F32),
        ),
        in_specs=[smem, hbm, hbm, hbm, hbm, hbm],
        out_specs=(vmem, vmem),
        scratch_shapes=[
            pltpu.SMEM((1, SPAN), jnp.int32),
            pltpu.SMEM((1, SPAN), jnp.int32),
            pltpu.SMEM((SPAN, GROUPS), jnp.int32),
            pltpu.VMEM((WINDOWS, CHANNELS, SAMPLES), BF16),
            pltpu.VMEM((4 * BAND, SAMPLES), BF16),
            pltpu.VMEM((BAND * CHUNK, CHANNELS), F32),
            pltpu.SemaphoreType.DMA((3,)),
            pltpu.SemaphoreType.DMA,
            pltpu.SemaphoreType.DMA,
        ],
        compiler_params=pltpu.CompilerParams(vmem_limit_bytes=32 << 20),
        name="whiten",
    )(
        place,
        *(
            pltpu.with_memory_space_constraint(operand, pltpu.HBM)
            for operand in (pair_listed, owner_slot, window_count[0], traces[0], band_table())
        ),
    )
    chunks = chunks.reshape(BAND, CHUNK // 2, 2, CHANNELS)
    chunks = lax.all_to_all(chunks, PLANE, 0, 0, tiled=True)
    chunks = chunks.reshape(BAND * CHUNK, CHANNELS)
    slots = pl.pallas_call(
        cross_kernel,
        out_shape=jax.ShapeDtypeStruct((GROUPS * BLOCKS * 2, OFFSETS), BF16),
        in_specs=[vmem] * 6,
        out_specs=vmem,
        scratch_shapes=[
            pltpu.VMEM((BAND * CHUNK, CHANNELS), F32),
            pltpu.VMEM((4, PLANE_GROUPS * WINDOWS * EXTENDED, 128), F32),
            pltpu.VMEM((SPAN * BLOCKS, 512), F32),
        ],
        compiler_params=pltpu.CompilerParams(vmem_limit_bytes=32 << 20),
        name="cross",
    )(chunks, *channel_table(), *offset_table(), order_table())
    slots = slots.reshape(GROUPS * BLOCKS, 2, OFFSETS)
    slots = lax.all_to_all(slots, WHOLE, 0, 0, tiled=True)
    slots = slots.reshape(GROUPS * BLOCKS * 2, OFFSETS)
    stacked = pl.pallas_call(
        lag_kernel,
        out_shape=jax.ShapeDtypeStruct((OFFSETS, LAGS), F32),
        in_specs=[vmem] * 4,
        out_specs=vmem,
        compiler_params=pltpu.CompilerParams(vmem_limit_bytes=32 << 20),
        name="lag",
    )(slots, weight, *lag_table())
    return stacked[None, None]


def solution(mesh):
    fine = Mesh(mesh.devices.reshape(4, 2, 2, 8, 4), CHAN + TM)
    placed = (
        P(CHAN, TM, None, None),
        P(CHAN, None),
        P(CHAN, None),
        P(CHAN, None, None),
    )
    return jax.shard_map(
        shards, mesh=fine, in_specs=placed, out_specs=P(CHAN, TM, None, None), check_vma=False
    )
```

```python
import math

import jax
import jax.numpy as jnp
import ml_dtypes
import numpy as np
from jax import lax
from jax.experimental import pallas as pl
from jax.experimental.pallas import tpu as pltpu
from jax.sharding import Mesh
from jax.sharding import PartitionSpec as P

BAND = 64
SMOOTH = 16
OFFSETS = 128
LAGS = 128
WATER = 0.1
CHANNELS = 128
SAMPLES = 512
PADDED = 192
WINDOWS = 4
BLOCKS = 16
GROUPS = 32
SPAN = 8
PLANE_GROUPS = 4
CHUNK = 10
EXTENDED = BLOCKS + SPAN

CHAN = ("x", "yh", "core")
TM = ("z", "yl")
PLANE = ("yl",) + CHAN
WHOLE = TM + CHAN
F32 = jnp.float32
BF16 = jnp.bfloat16


def angles(left, right, period):
    return 2.0 * np.pi / period * ((left[:, None] * right[None, :]) % period)


def split_table(table):
    table = table.astype(np.float32)
    high = table.astype(ml_dtypes.bfloat16)
    low = (table - high.astype(np.float32)).astype(ml_dtypes.bfloat16)
    return high, low


def band_table():
    turn = angles(np.arange(BAND) + 1, np.arange(SAMPLES), SAMPLES)
    high, low = split_table(np.concatenate([np.cos(turn), -np.sin(turn)], axis=0))
    return np.concatenate([high, low], axis=0)


def channel_table():
    turn = angles(np.arange(CHANNELS), np.arange(PADDED), PADDED)
    real_part = np.concatenate([np.cos(turn), np.sin(turn)], axis=0)
    imag_part = np.concatenate([-np.sin(turn), np.cos(turn)], axis=0)
    real_rest, imag_rest = real_part[:, 128:], imag_part[:, 128:]
    return split_table(
        np.concatenate(
            [real_part[:, :128], imag_part[:, :128], real_rest, imag_rest, imag_rest, real_rest],
            axis=1,
        )
    )


def offset_table():
    turn = angles(np.arange(PADDED), np.arange(OFFSETS) - OFFSETS // 2, PADDED)
    of_real = np.concatenate([np.cos(turn), np.sin(turn)], axis=1) / PADDED
    of_imag = np.concatenate([-np.sin(turn), np.cos(turn)], axis=1) / PADDED
    real_rest, imag_rest = of_real[128:], of_imag[128:]
    return split_table(
        np.concatenate(
            [of_real[:128], of_imag[:128], real_rest, real_rest, imag_rest, -imag_rest], axis=0
        )
    )


def lag_table():
    turn = angles(np.arange(BAND) + 1, np.arange(LAGS) - LAGS // 2, SAMPLES)
    pair = np.stack([np.cos(turn), -np.sin(turn)], axis=1).reshape(2 * BAND, LAGS)
    return split_table(pair / math.sqrt(BAND))


def dot(left, right):
    return jnp.dot(left, right, preferred_element_type=F32)


def split(value):
    high = value.astype(BF16)
    return high, (value - high.astype(F32)).astype(BF16)


def dot_split(value, table_high, table_low):
    high, low = split(value)
    return dot(high, table_high) + (dot(low, table_high) + dot(high, table_low))


def smooth_matrix():
    target = lax.broadcasted_iota(jnp.int32, (2 * BAND, 2 * BAND), 0)
    source = lax.broadcasted_iota(jnp.int32, (2 * BAND, 2 * BAND), 1)
    source = jnp.where(source >= BAND, source - BAND, source)
    start = jnp.clip(target - SMOOTH // 2, 0, BAND - SMOOTH)
    inside = (target >= BAND) | ((source >= start) & (source < start + SMOOTH))
    return inside.astype(F32).astype(BF16)


def whiten_kernel(
    place,
    listed_hbm,
    owners_hbm,
    counts_hbm,
    traces_hbm,
    table_hbm,
    out,
    weight,
    listed,
    owners,
    counts,
    traces,
    table,
    rows,
    smooth,
    small_sems,
    table_sem,
    trace_sem,
):
    small = [
        pltpu.make_async_copy(source, target, small_sems.at[k])
        for k, (source, target) in enumerate(
            ((listed_hbm, listed), (owners_hbm, owners), (counts_hbm, counts))
        )
    ]
    whole_table = pltpu.make_async_copy(table_hbm, table, table_sem)
    whole_traces = pltpu.make_async_copy(traces_hbm, traces, trace_sem)
    whole_table.start()
    whole_traces.start()
    for copy in small:
        copy.start()
    for copy in small:
        copy.wait()
    lane = lax.broadcasted_iota(jnp.int32, (8, CHANNELS), 1)
    count_row = jnp.zeros((8, CHANNELS), jnp.int32)
    owner_row = jnp.zeros((8, CHANNELS), jnp.int32)
    mine = jnp.int32(0)
    found = jnp.int32(0)
    for step in range(SPAN):
        owner = owners[0, step]
        count_row = jnp.where(lane == step, counts[step, place[0]], count_row)
        owner_row = jnp.where(lane == step, owner, owner_row)
        here = owner == place[0]
        mine = jnp.where(here, step, mine)
        found = jnp.where(here, listed[0, step], found)
    total = jnp.int32(0)
    for group in range(GROUPS):
        total = total + counts[mine, group]
    weight[...] = jnp.full((8, LAGS), found, jnp.int32).astype(F32) / jnp.full(
        (8, LAGS), total, jnp.int32
    ).astype(F32)
    count_row = count_row.astype(F32)
    owner_row = owner_row.astype(F32)
    for part in range(BAND // 8):
        rows[pl.ds(part * 8 * CHUNK + 8, 8, stride=CHUNK), :] = count_row
        rows[pl.ds(part * 8 * CHUNK + 9, 8, stride=CHUNK), :] = owner_row
    smooth[...] = smooth_matrix()
    whole_table.wait()
    whole_traces.wait()
    flat = traces[...].reshape(WINDOWS * CHANNELS, SAMPLES)
    both = lax.dot_general(
        table[...], flat, (((1,), (1,)), ((), ())), preferred_element_type=F32
    )
    spectrum = both[: 2 * BAND] + both[2 * BAND :]
    real_part = spectrum[:BAND]
    imag_part = spectrum[BAND:]
    amplitude = jnp.sqrt(real_part * real_part + imag_part * imag_part)
    sums = dot(smooth[...], jnp.concatenate(split(amplitude), axis=0))
    water_level = sums[:BAND] / SMOOTH + WATER * (sums[BAND:] / BAND) + 1e-6
    real_part = real_part / water_level
    imag_part = imag_part / water_level
    for window in range(WINDOWS):
        here = slice(window * CHANNELS, (window + 1) * CHANNELS)
        rows[pl.ds(window, BAND, stride=CHUNK), :] = real_part[:, here]
        rows[pl.ds(WINDOWS + window, BAND, stride=CHUNK), :] = imag_part[:, here]
    out[...] = rows[...].astype(BF16)


def cross_kernel(
    chunks, to_high, to_low, back_high, back_low, out, rows, spectra, cross, pieces, named
):
    rows[...] = chunks[...].astype(F32)
    block_rows = BLOCKS * CHUNK
    block_data = jnp.concatenate(
        [
            jnp.concatenate(
                [
                    rows[pl.ds(group * block_rows + part * WINDOWS + window, BLOCKS, stride=CHUNK), :]
                    for part in range(2)
                ],
                axis=1,
            ).astype(BF16)
            for group in range(PLANE_GROUPS)
            for window in range(WINDOWS)
        ],
        axis=0,
    )
    both = dot(block_data, to_high[...]) + dot(block_data, to_low[...])
    for tile in range(4):
        lanes = slice(tile * 128, (tile + 1) * 128)
        for window in range(PLANE_GROUPS * WINDOWS):
            source, target = window * BLOCKS, window * EXTENDED
            spectra[tile, target : target + SPAN, :] = both[source + SPAN : source + BLOCKS, lanes]
            spectra[tile, target + SPAN : target + EXTENDED, :] = both[
                source : source + BLOCKS, lanes
            ]
    counts = [
        rows[pl.ds(group * block_rows + 8, 16, stride=CHUNK), :] for group in range(PLANE_GROUPS)
    ]
    owners = rows[pl.ds(9, 16, stride=CHUNK), :]
    for step in range(SPAN):
        distance = step + 1
        limits = [
            jnp.broadcast_to(counts[group][:, step : step + 1], (BLOCKS, 128))
            for group in range(PLANE_GROUPS)
        ]
        here = slice(step * BLOCKS, (step + 1) * BLOCKS)
        for half in range(2):
            first = jnp.zeros((BLOCKS, 128), F32)
            second = jnp.zeros((BLOCKS, 128), F32)
            for group in range(PLANE_GROUPS):
                for window in range(WINDOWS):
                    base = (group * WINDOWS + window) * EXTENDED + SPAN
                    own = slice(base, base + BLOCKS)
                    before = slice(base - distance, base - distance + BLOCKS)
                    keep = limits[group] > float(window)
                    if half == 0:
                        own_real = spectra[0, own, :]
                        own_imag = spectra[1, own, :]
                        src_real = spectra[0, before, :]
                        src_imag = spectra[1, before, :]
                        if window > 0:
                            src_real = jnp.where(keep, src_real, 0.0)
                            src_imag = jnp.where(keep, src_imag, 0.0)
                        first = first + (src_real * own_real + src_imag * own_imag)
                        second = second + (src_real * own_imag - src_imag * own_real)
                    else:
                        source = spectra[2, before, :]
                        if window > 0:
                            source = jnp.where(keep, source, 0.0)
                        first = first + source * spectra[2, own, :]
                        second = second + source * spectra[3, own, :]
            cross[here, half * 256 : half * 256 + 128] = first
            cross[here, half * 256 + 128 : half * 256 + 256] = second
        chosen = jnp.broadcast_to(owners[:, step : step + 1], (BLOCKS, 128))
        for half in range(2):
            named[pl.ds(step * 2 * BLOCKS + half, BLOCKS, stride=2), :] = chosen
    high, low = split(cross[...])
    pairs = SPAN * BLOCKS
    by_high = dot(jnp.concatenate([high, low], axis=0), back_high[...])
    partial = by_high[:pairs] + (by_high[pairs:] + dot(high, back_low[...]))
    for half in range(2):
        pieces[pl.ds(half, pairs, stride=2), :] = partial[:, half * 128 : (half + 1) * 128]
    lines = 2 * BLOCKS
    piece_of = [
        pieces[step * lines : (step + 1) * lines, :].astype(BF16) for step in range(SPAN)
    ]
    owner_of = [
        named[step * lines : (step + 1) * lines, :].astype(BF16) for step in range(SPAN)
    ]
    for owner in range(GROUPS):
        chunk = jnp.zeros((lines, OFFSETS), BF16)
        for step in range(SPAN):
            chunk = jnp.where(owner_of[step] == jnp.bfloat16(owner), piece_of[step], chunk)
        out[owner * lines : (owner + 1) * lines, :] = chunk


def lag_kernel(arrived, weight, table_high, table_low, out):
    summed = arrived[: 2 * BAND].astype(F32)
    for layer in range(1, 8):
        summed = summed + arrived[layer * 2 * BAND : (layer + 1) * 2 * BAND].astype(F32)
    lagged = dot_split(summed.T, table_high[...], table_low[...])
    out[...] = lagged * weight[:1]


def shards(traces, pair_listed, owner_slot, window_count):
    vmem = pl.BlockSpec(memory_space=pltpu.VMEM)
    smem = pl.BlockSpec(memory_space=pltpu.SMEM)
    place = lax.axis_index(TM).astype(jnp.int32).reshape(1)
    hbm = pl.BlockSpec(memory_space=pltpu.HBM)
    chunks, weight = pl.pallas_call(
        whiten_kernel,
        out_shape=(
            jax.ShapeDtypeStruct((BAND * CHUNK, CHANNELS), BF16),
            jax.ShapeDtypeStruct((8, LAGS), F32),
        ),
        in_specs=[smem, hbm, hbm, hbm, hbm, hbm],
        out_specs=(vmem, vmem),
        scratch_shapes=[
            pltpu.SMEM((1, SPAN), jnp.int32),
            pltpu.SMEM((1, SPAN), jnp.int32),
            pltpu.SMEM((SPAN, GROUPS), jnp.int32),
            pltpu.VMEM((WINDOWS, CHANNELS, SAMPLES), BF16),
            pltpu.VMEM((4 * BAND, SAMPLES), BF16),
            pltpu.VMEM((BAND * CHUNK, CHANNELS), F32),
            pltpu.VMEM((2 * BAND, 2 * BAND), BF16),
            pltpu.SemaphoreType.DMA((3,)),
            pltpu.SemaphoreType.DMA,
            pltpu.SemaphoreType.DMA,
        ],
        compiler_params=pltpu.CompilerParams(vmem_limit_bytes=32 << 20),
        name="whiten",
    )(
        place,
        *(
            pltpu.with_memory_space_constraint(operand, pltpu.HBM)
            for operand in (pair_listed, owner_slot, window_count[0], traces[0], band_table())
        ),
    )
    chunks = chunks.reshape(BAND, CHUNK // 2, 2, CHANNELS)
    chunks = lax.all_to_all(chunks, PLANE, 0, 0, tiled=True)
    chunks = chunks.reshape(BAND * CHUNK, CHANNELS)
    slots = pl.pallas_call(
        cross_kernel,
        out_shape=jax.ShapeDtypeStruct((GROUPS * BLOCKS * 2, OFFSETS), BF16),
        in_specs=[vmem] * 5,
        out_specs=vmem,
        scratch_shapes=[
            pltpu.VMEM((BAND * CHUNK, CHANNELS), F32),
            pltpu.VMEM((4, PLANE_GROUPS * WINDOWS * EXTENDED, 128), F32),
            pltpu.VMEM((SPAN * BLOCKS, 512), F32),
            pltpu.VMEM((SPAN * BLOCKS * 2, OFFSETS), F32),
            pltpu.VMEM((SPAN * BLOCKS * 2, OFFSETS), F32),
        ],
        compiler_params=pltpu.CompilerParams(vmem_limit_bytes=32 << 20),
        name="cross",
    )(chunks, *channel_table(), *offset_table())
    slots = slots.reshape(GROUPS * BLOCKS, 2, OFFSETS)
    slots = lax.all_to_all(slots, WHOLE, 0, 0, tiled=True)
    slots = slots.reshape(GROUPS * BLOCKS * 2, OFFSETS)
    stacked = pl.pallas_call(
        lag_kernel,
        out_shape=jax.ShapeDtypeStruct((OFFSETS, LAGS), F32),
        in_specs=[vmem] * 4,
        out_specs=vmem,
        compiler_params=pltpu.CompilerParams(vmem_limit_bytes=32 << 20),
        name="lag",
    )(slots, weight, *lag_table())
    return stacked[None, None]


def solution(mesh):
    fine = Mesh(mesh.devices.reshape(4, 2, 2, 8, 4), CHAN + TM)
    placed = (
        P(CHAN, TM, None, None),
        P(CHAN, None),
        P(CHAN, None),
        P(CHAN, None, None),
    )
    return jax.shard_map(
        shards, mesh=fine, in_specs=placed, out_specs=P(CHAN, TM, None, None), check_vma=False
    )
```
